32 devices in a mesh: col: 8 (over z, x), row: 4 (over y, core).
Axes of the slice: x: 2, y: 2, z: 4, core: 2. Of those that a mesh axis runs over, the one named last changes fastest.
Arguments:
- returns: bfloat16 [4096, 2048], P(('row', 'col')), may hold values from -6 to 6
- counts: int32 [4096], P(('row', 'col')), may hold values from 0 to 4
- partner_shift: int32 [3], replicated, may hold values from 1 to 7
Outputs:
- blocks_out: float32 [4096, 2048], P('row', 'col')
- bounds: float32 [3], replicated
The draws below stay inside these ranges and needn't reach their ends.
All inputs are finite; a program needn't handle non-finite values.
Results may differ from the reference program's by a relative error of at most 0.0003.
Values sent between devices are 32-bit elements; how exact they have to be, the bound alone decides.
No kernel may reach another device: no remote copies, remote signals or barrier semaphores. Data moves between devices by JAX's collectives and lax.ppermute only.
A program may use at most 128 MiB of HBM per device.

```python
import jax
import jax.numpy as jnp
from jax import lax

BW = 128
ROUNDS = 3
DAYS = 4096
SERIES = 2048
N_COL = 8


def touch_ends(entries, stream_key, least, high):
    longest = entries.shape.index(max(entries.shape))
    spots = []
    for shift in (0, 1):
        where = [jax.random.randint(jax.random.fold_in(stream_key, axis), (), 0, length) for axis, length in enumerate(entries.shape)]
        where[longest] = (where[longest] + shift) % entries.shape[longest]
        spots.append(tuple(where))
    return entries.at[spots[0]].set(least).at[spots[1]].set(high)


def shard_levels(own_key, shape, pieces, least, top_value):
    loudness, own = 1.0, jax.random.fold_in(own_key, 6)
    for position, shards_of in pieces:
        draws = jnp.exp(jax.random.uniform(jax.random.fold_in(own, position), (shards_of,), jnp.float32, least / len(pieces), top_value / len(pieces)))
        loudness = loudness * jnp.repeat(draws, shape[position] // shards_of).reshape([-1 if axis == position else 1 for axis in range(len(shape))])
    return loudness


def noise(own_key, shape, scale, reach, cuts=(), held_as=jnp.bfloat16):
    values = scale * jax.random.normal(own_key, shape, jnp.float32)
    if cuts:
        values = values * shard_levels(own_key, shape, cuts, -0.22, 0.18)
    return jnp.clip(values, -reach, reach).astype(held_as)


def setup_inputs(seed: int = 0) -> dict:
    arg_keys = jax.random.split(jax.random.key(seed), 4)
    return {
        "returns": noise(arg_keys[0], (DAYS, SERIES), 1.0, 6.0, ((0, 32),)),
        "counts": touch_ends(jax.random.randint(arg_keys[1], (DAYS,), 0, 5), jax.random.fold_in(arg_keys[1], 1), 0, 4).astype(jnp.int32),
        "partner_shift": jax.random.randint(arg_keys[2], (ROUNDS,), 1, N_COL).astype(jnp.int32),
    }


HIGH = lax.Precision.HIGHEST

def coupling_of(gram):
    width = gram.shape[0] // 2
    norms = jnp.sqrt(jnp.diagonal(gram) / DAYS + 1e-06)
    return gram[:width, width:] / (DAYS * norms[:width, None] * norms[None, width:])

def rotation(coupling, top):
    width = coupling.shape[0]
    zeros = jnp.zeros((width, width), jnp.float32)
    skew = jnp.concatenate([jnp.concatenate([zeros, coupling], 1), jnp.concatenate([-coupling.T, zeros], 1)], 0)
    factor = (jnp.eye(2 * width, dtype=jnp.float32) + skew) / jnp.sqrt(1.0 + top)
    for step in range(3):
        inner = jnp.dot(factor.T, factor, precision=HIGH)
        factor = 1.5 * factor - 0.5 * jnp.dot(factor, inner, precision=HIGH)
    return factor

def reference(returns, counts, partner_shift):
    weighted = returns.astype(jnp.float32) * jnp.sqrt(counts.astype(jnp.float32))[:, None]
    pairs = weighted.reshape(DAYS, N_COL, 2 * BW).transpose(1, 0, 2)
    bounds = []
    for rnd in range(ROUNDS):
        gram = jnp.einsum('cdi,cdj->cij', pairs, pairs, precision=HIGH)
        coupling = jax.vmap(coupling_of)(gram)
        top = jnp.max(lax.optimization_barrier(jnp.sum(coupling * coupling, axis=(1, 2))))
        bounds.append(top)
        factors = jax.vmap(rotation, in_axes=(0, None))(coupling, top)
        rotated = jnp.einsum('cdi,cij->cdj', pairs, factors, precision=HIGH)
        moving = jnp.roll(rotated[:, :, BW:], partner_shift[rnd], axis=0)
        pairs = jnp.concatenate([rotated[:, :, :BW], moving], axis=2)
    blocks_out = pairs.transpose(1, 0, 2).reshape(DAYS, 2 * BW * N_COL)
    return (blocks_out, jnp.stack(bounds))
```

```python
import jax
import jax.numpy as jnp
from jax import lax
from jax.sharding import PartitionSpec as P

BW = 128
ROUNDS = 3
RADIX = 8
HIGH = lax.Precision.HIGH


def dot(a, b):
    return jnp.dot(a, b, precision=HIGH)


def forward(x, hop):
    n = lax.axis_size("col")
    return lax.ppermute(x, "col", [(i, (i + hop) % n) for i in range(n)])


def swapped(x, axis, mask):
    return lax.ppermute(x, axis, [(i, i ^ mask) for i in range(lax.axis_size(axis))])


def row_sum(x):
    parts = [x] + [swapped(x, "row", m) for m in range(1, lax.axis_size("row"))]
    while len(parts) > 1:
        parts = [parts[i] + parts[i + 1] for i in range(0, len(parts), 2)]
    return parts[0]


def col_max(x):
    mask = 1
    while mask < lax.axis_size("col"):
        x = jnp.maximum(x, swapped(x, "col", mask))
        mask *= 2
    return x


def to_pairs(weighted):
    n = lax.axis_size("col")
    if n > RADIX:
        return lax.all_to_all(weighted, "col", split_axis=1, concat_axis=0, tiled=True)
    me = lax.axis_index("col")
    days, width = weighted.shape[0], weighted.shape[1] // n
    pair = jnp.zeros((days * n, width), jnp.float32)
    for hop in [4, 3, 5, 2, 6, 1, 7, 0]:
        if hop >= n:
            continue
        block = lax.dynamic_slice(weighted, (0, (me + hop) % n * width), (days, width))
        block = forward(block, hop) if hop else block
        pair = lax.dynamic_update_slice(pair, block, ((me - hop) % n * days, 0))
    return pair


def polar(m, top):
    eye = jnp.eye(m.shape[0], dtype=jnp.float32)
    square = 1.0 / (1.0 + top)
    gram = square * (eye + m)
    t0 = 1.5 * eye - 0.5 * gram
    gram = dot(gram, dot(t0, t0))
    t1 = 1.5 * eye - 0.5 * gram
    gram = dot(gram, dot(t1, t1))
    t2 = 1.5 * eye - 0.5 * gram
    return jnp.sqrt(square) * dot(dot(t0, t1), t2)


def on_device(returns, counts, partner_shift):
    n = lax.axis_size("col")
    days = returns.shape[0] * n * lax.axis_size("row")
    weighted = returns.astype(jnp.float32) * jnp.sqrt(counts.astype(jnp.float32))[:, None]
    pair = to_pairs(weighted)
    first, second = pair[:, :BW], pair[:, BW:]
    strides = [1]
    while strides[-1] * RADIX < n:
        strides.append(strides[-1] * RADIX)
    lowest = 1 if len(strides) == 1 else 0
    bounds = []
    for rnd in range(ROUNDS):
        cross = dot(first.T, second)
        squares = jnp.stack([jnp.sum(first * first, 0), jnp.sum(second * second, 0)])
        summed = row_sum(jnp.concatenate([cross, squares, jnp.zeros((6, BW), jnp.float32)], 0))
        norms = jnp.sqrt(summed[BW:BW + 2] / days + 1e-06)
        coupling = summed[:BW] / (days * norms[0][:, None] * norms[1][None, :])
        measure = jnp.sum(coupling * coupling)
        mixed = dot(first, coupling) + second

        def move(hop, first, second, mixed, coupling, measure):
            there = forward(coupling, hop) if hop else coupling
            mixed = forward(mixed, hop) if hop else mixed
            top = col_max(jnp.broadcast_to(measure, (8, BW)))[0, 0]
            kept = dot(first - dot(second, coupling.T), polar(dot(coupling, coupling.T), top))
            return kept, mixed, polar(dot(there.T, there), top), top

        amount = partner_shift[rnd]
        branches = [
            lambda *a, hop=hop: move(hop, *a) for hop in range(lowest, min(n, RADIX))
        ]
        first, mixed, factor, top = lax.switch(
            amount % RADIX - lowest, branches, first, second, mixed, coupling, measure
        )
        for stride in strides[1:]:
            routes = [lambda *a: a] + [
                lambda *a, hop=hop: tuple(forward(v, hop * stride) for v in a)
                for hop in range(1, min(RADIX, n // stride))
            ]
            mixed, factor = lax.switch(amount // stride % RADIX, routes, mixed, factor)
        second = dot(mixed, factor)
        bounds.append(top)
    return jnp.concatenate([first, second], 1), jnp.stack(bounds)


def solution(mesh):
    placed = (P(("row", "col"), None), P(("row", "col")), P())
    return jax.shard_map(
        on_device, mesh=mesh, in_specs=placed, out_specs=(P("row", "col"), P()), check_vma=False
    )
```

```python
import functools

import jax
import jax.numpy as jnp
from jax import lax
from jax.experimental import pallas as pl
from jax.experimental.pallas import tpu as pltpu
from jax.sharding import PartitionSpec as P

BW = 128
ROUNDS = 3
RADIX = 8
TILE = 8
F32 = jnp.float32


def split(x):
    high = x.astype(jnp.bfloat16)
    return high, (x - high.astype(F32)).astype(jnp.bfloat16)


def dot(a, b, dims=((1,), (0,))):
    one = functools.partial(
        lax.dot_general, dimension_numbers=(dims, ((), ())), preferred_element_type=F32
    )
    return one(a[0], b[0]) + (one(a[0], b[1]) + one(a[1], b[0]))


def dots(a, b, dims=((1,), (0,))):
    return dot(split(a), split(b), dims)


def unit():
    rows = lax.broadcasted_iota(jnp.int32, (BW, BW), 0)
    return (rows == lax.broadcasted_iota(jnp.int32, (BW, BW), 1)).astype(F32)


def polar(m, top):
    eye = unit()
    square = 1.0 / (1.0 + top)
    gram = square * (eye + m)
    t0 = 1.5 * eye - 0.5 * gram
    s0 = split(t0)
    gram = dot(split(gram), split(dot(s0, s0)))
    t1 = 1.5 * eye - 0.5 * gram
    s1 = split(t1)
    gram = dot(split(gram), split(dot(s1, s1)))
    t2 = 1.5 * eye - 0.5 * gram
    return jnp.sqrt(square) * dot(split(dot(s0, s1)), split(t2))


def gram_into(first, second, gram_ref):
    gram_ref[:BW] = dots(first, second, ((0,), (0,)))
    gram_ref[BW:BW + 1] = jnp.sum(first * first, 0, keepdims=True)
    gram_ref[BW + 1:BW + 2] = jnp.sum(second * second, 0, keepdims=True)
    gram_ref[BW + 2:] = jnp.zeros((TILE - 2, BW), F32)


def gather_kernel(at_ref, *refs):
    blocks, (first_ref, second_ref, gram_ref) = refs[:-3], refs[-3:]
    days = blocks[0].shape[0]
    for i, block in enumerate(blocks):
        place = pl.ds(pl.multiple_of(at_ref[i] * days, TILE), days)
        first_ref[place] = block[:, :BW]
        second_ref[place] = block[:, BW:]
    gram_into(first_ref[...], second_ref[...], gram_ref)


def couple_kernel(total_days, g0, g1, g2, g3, first, second, load_ref, measure_ref):
    summed = (g0[...] + g1[...]) + (g2[...] + g3[...])
    norms = jnp.sqrt(summed[BW:BW + 2] / total_days + 1e-06)
    across = jnp.broadcast_to(norms[1:2], (BW, BW))
    down = jnp.broadcast_to(norms[0:1], (BW, BW)).T
    coupling = summed[:BW] / (total_days * down * across)
    measure_ref[...] = jnp.full((TILE, BW), jnp.sum(coupling * coupling), F32)
    load_ref[:BW] = coupling
    load_ref[BW:] = dots(first[...], coupling) + second[...]


def keep_kernel(m0, m1, m2, m3, load, first, second, first_ref, top_ref):
    top = jnp.maximum(jnp.maximum(m0[...], m1[...]), jnp.maximum(m2[...], m3[...]))
    top_ref[...] = top
    coupling = load[:BW]
    cut = split(coupling)
    factor = polar(dot(cut, cut, ((1,), (1,))), top[:1])
    weight = split(factor)
    other = split(dot(cut, weight, ((0,), (0,))))
    first_ref[...] = dot(split(first[...]), weight) - dot(split(second[...]), other)


def arrived(load, top):
    cut = split(load[:BW])
    return dots(load[BW:], polar(dot(cut, cut, ((0,), (0,))), top[:1]))


def next_kernel(load, first, top, second_ref, gram_ref):
    second = arrived(load, top)
    second_ref[...] = second
    gram_into(first[...], second, gram_ref)


def last_kernel(load, first, top0, top1, top2, out_ref, bounds_ref):
    out_ref[:, :BW] = first[...]
    out_ref[:, BW:] = arrived(load, top2)
    for i, top in enumerate((top0, top1, top2)):
        bounds_ref[i] = jnp.max(top[...])


def call(kernel, outs, *args, smem_in=0, smem_out=0):
    vmem, smem = pl.BlockSpec(memory_space=pltpu.VMEM), pl.BlockSpec(memory_space=pltpu.SMEM)
    shapes = [jax.ShapeDtypeStruct(s, F32) for s in outs]
    return pl.pallas_call(
        kernel,
        out_shape=shapes,
        in_specs=[smem] * smem_in + [vmem] * (len(args) - smem_in),
        out_specs=[vmem] * (len(outs) - smem_out) + [smem] * smem_out,
        compiler_params=pltpu.CompilerParams(vmem_limit_bytes=24 << 20),
    )(*args)


def forward(x, hop):
    n = lax.axis_size("col")
    return lax.ppermute(x, "col", [(i, (i + hop) % n) for i in range(n)])


def swapped(x, axis, mask):
    return lax.ppermute(x, axis, [(i, i ^ mask) for i in range(lax.axis_size(axis))])


def row_parts(x):
    return [x] + [swapped(x, "row", m) for m in range(1, lax.axis_size("row"))]


def most_of_col(x):
    n, rows = lax.axis_size("col"), lax.axis_size("row")
    mask = RADIX
    while mask < n:
        x = jnp.maximum(x, swapped(x, "col", mask))
        mask *= 2
    near = min(n, RADIX) - 1
    each = -(-near // rows)
    seen = []
    for j in range(each):
        route = [
            (c * rows + r, (c ^ min(1 + r * each + j, near)) * rows + r)
            for r in range(rows) for c in range(n)
        ]
        seen.append(lax.ppermute(x, ("col", "row"), route))
    return functools.reduce(jnp.maximum, seen, x)


def to_pairs(weighted):
    n = lax.axis_size("col")
    if n > RADIX:
        whole = lax.all_to_all(weighted, "col", split_axis=1, concat_axis=0, tiled=True)
        return [whole], jnp.zeros((1,), jnp.int32)
    me = lax.axis_index("col")
    days, width = weighted.shape[0], weighted.shape[1] // n
    hops = sorted(range(n), key=lambda h: -min(h, n - h))
    blocks = []
    for hop in hops:
        block = lax.dynamic_slice(weighted, (0, (me + hop) % n * width), (days, width))
        blocks.append(forward(block, hop) if hop else block)
    return blocks, jnp.stack([(me - hop) % n for hop in hops]).astype(jnp.int32)


def on_device(returns, counts, partner_shift):
    n, rows = lax.axis_size("col"), lax.axis_size("row")
    total_days = returns.shape[0] * n * rows
    mine = total_days // rows
    weighted = returns.astype(F32) * jnp.sqrt(counts.astype(F32))[:, None]
    blocks, at = to_pairs(weighted)
    block, gram_shape, tile = (mine, BW), (BW + TILE, BW), (TILE, BW)
    first, second, gram = call(
        gather_kernel, [block, block, gram_shape], at, *blocks, smem_in=1
    )
    strides = [1]
    while strides[-1] * RADIX < n:
        strides.append(strides[-1] * RADIX)
    lowest = 1 if len(strides) == 1 else 0
    tops = []
    for rnd in range(ROUNDS):
        load, measure = call(
            functools.partial(couple_kernel, float(total_days)), [(BW + mine, BW), tile],
            *row_parts(gram), first, second,
        )

        def move(hop, first, second, load, measure):
            part = most_of_col(measure)
            moved = forward(load, hop) if hop else load
            kept, top = call(keep_kernel, [block, tile], *row_parts(part), load, first, second)
            return kept, moved, top

        amount = partner_shift[rnd]
        branches = [functools.partial(move, hop) for hop in range(lowest, min(n, RADIX))]
        first, load, top = lax.switch(
            amount % RADIX - lowest, branches, first, second, load, measure
        )
        for stride in strides[1:]:
            routes = [lambda x: x] + [
                functools.partial(forward, hop=hop * stride)
                for hop in range(1, min(RADIX, n // stride))
            ]
            load = lax.switch(amount // stride % RADIX, routes, load)
        tops.append(top)
        if rnd < ROUNDS - 1:
            second, gram = call(next_kernel, [block, gram_shape], load, first, top)
    return tuple(call(last_kernel, [(mine, 2 * BW), (ROUNDS,)], load, first, *tops, smem_out=1))


def solution(mesh):
    placed = (P(("row", "col"), None), P(("row", "col")), P())
    return jax.shard_map(
        on_device, mesh=mesh, in_specs=placed, out_specs=(P("row", "col"), P()), check_vma=False
    )
```

```python
import functools

import jax
import jax.numpy as jnp
from jax import lax
from jax.experimental import pallas as pl
from jax.experimental.pallas import tpu as pltpu
from jax.sharding import PartitionSpec as P

BW = 128
ROUNDS = 3
RADIX = 8
TILE = 8
LONG = 3 << 30
STEP = 256
F32 = jnp.float32


def split(x):
    high = x.astype(jnp.bfloat16)
    return high, (x - high.astype(F32)).astype(jnp.bfloat16)


def dot(a, b, dims=((1,), (0,))):
    one = functools.partial(
        lax.dot_general, dimension_numbers=(dims, ((), ())), preferred_element_type=F32
    )
    return one(a[0], b[0]) + (one(a[0], b[1]) + one(a[1], b[0]))


def dots(a, b, dims=((1,), (0,))):
    return dot(split(a), split(b), dims)


def unit():
    rows = lax.broadcasted_iota(jnp.int32, (BW, BW), 0)
    return (rows == lax.broadcasted_iota(jnp.int32, (BW, BW), 1)).astype(F32)


def polar(m, top):
    eye = unit()
    square = 1.0 / (1.0 + top)
    gram, product = square * (eye + m), None
    for turn in range(3):
        factor = 1.5 * eye - 0.5 * gram
        cut = split(factor)
        product = factor if product is None else dot(split(product), cut)
        if turn < 2:
            gram = dot(split(gram), split(dot(cut, cut)))
    return jnp.sqrt(square) * product


def steps(size, body):
    @pl.loop(0, size // STEP)
    def _(i):
        body(i * STEP, pl.ds(pl.multiple_of(i * STEP, STEP), STEP))


def gram_into(first, second, gram_ref):
    gram_ref[:BW] += dots(first, second, ((0,), (0,)))
    gram_ref[BW:BW + 1] += jnp.sum(first * first, 0, keepdims=True)
    gram_ref[BW + 1:BW + 2] += jnp.sum(second * second, 0, keepdims=True)


def gather_kernel(at_ref, *refs):
    blocks, (first_ref, second_ref, gram_ref) = refs[:-3], refs[-3:]
    days = blocks[0].shape[0]
    for i, block in enumerate(blocks):
        place = pl.ds(pl.multiple_of(at_ref[i] * days, TILE), days)
        first_ref[place] = block[:, :BW]
        second_ref[place] = block[:, BW:]
    gram_ref[...] = jnp.zeros_like(gram_ref)
    gram_into(first_ref[...], second_ref[...], gram_ref)


def couple_kernel(total_days, g0, g1, g2, g3, coupling_ref, measure_ref):
    summed = (g0[...] + g1[...]) + (g2[...] + g3[...])
    norms = jnp.sqrt(summed[BW:BW + 2] / total_days + 1e-06)
    across = jnp.broadcast_to(norms[1:2], (BW, BW))
    down = jnp.broadcast_to(norms[0:1], (BW, BW)).T
    coupling = summed[:BW] / (total_days * down * across)
    measure_ref[...] = jnp.full((TILE, BW), jnp.sum(coupling * coupling), F32)
    coupling_ref[...] = coupling


def early_mix_kernel(coupling, first, second, early_ref):
    lead = early_ref.shape[0] - BW
    early_ref[:BW] = coupling[...]
    early_ref[BW:] = dots(first[:lead], coupling[...]) + second[:lead]


def late_mix_kernel(coupling, first, second, late_ref):
    lead = first.shape[0] - late_ref.shape[0]
    cut = split(coupling[...])

    def body(at, here):
        there = pl.ds(pl.multiple_of(lead + at, STEP), STEP)
        late_ref[here] = dot(split(first[there]), cut) + second[there]

    steps(late_ref.shape[0], body)


def keep_kernel(m0, m1, m2, m3, coupling, first, second, first_ref, top_ref):
    top = jnp.maximum(jnp.maximum(m0[...], m1[...]), jnp.maximum(m2[...], m3[...]))
    top_ref[...] = top
    cut = split(coupling[...])
    factor = polar(dot(cut, cut, ((1,), (1,))), top[:1])
    weight = split(factor)
    other = split(dot(cut, weight, ((0,), (0,))))

    def body(_, here):
        first_ref[here] = dot(split(first[here]), weight) - dot(split(second[here]), other)

    steps(first.shape[0], body)


def early_kernel(early, first, top, factor_ref, second_ref, gram_ref):
    cut = split(early[:BW])
    factor = polar(dot(cut, cut, ((0,), (0,))), top[:1])
    factor_ref[...] = factor
    weight = split(factor)
    gram_ref[...] = jnp.zeros_like(gram_ref)

    def body(at, here):
        there = pl.ds(pl.multiple_of(BW + at, BW), STEP)
        second_ref[here] = dot(split(early[there]), weight)
        gram_into(first[here], second_ref[here], gram_ref)

    steps(second_ref.shape[0], body)


def late_kernel(late, factor, first, lead, gram, second_ref, gram_ref):
    second = dots(late[...], factor[...])
    size = lead.shape[0]
    second_ref[:size] = lead[...]
    second_ref[size:] = second
    gram_ref[...] = gram[...]
    gram_into(first[size:], second, gram_ref)


def last_kernel(late, factor, first, lead, top0, top1, top2, out_ref, bounds_ref):
    size = lead.shape[0]
    out_ref[:, :BW] = first[...]
    out_ref[:size, BW:] = lead[...]
    out_ref[size:, BW:] = dots(late[...], factor[...])
    for i, top in enumerate((top0, top1, top2)):
        bounds_ref[i] = jnp.max(top[...])


def call(kernel, outs, *args, smem_in=0, smem_out=0, flops=0):
    vmem, smem = pl.BlockSpec(memory_space=pltpu.VMEM), pl.BlockSpec(memory_space=pltpu.SMEM)
    shapes = [jax.ShapeDtypeStruct(s, F32) for s in outs]
    return pl.pallas_call(
        kernel,
        out_shape=shapes,
        in_specs=[smem] * smem_in + [vmem] * (len(args) - smem_in),
        out_specs=[vmem] * (len(outs) - smem_out) + [smem] * smem_out,
        compiler_params=pltpu.CompilerParams(vmem_limit_bytes=24 << 20),
        cost_estimate=pl.CostEstimate(flops=flops, bytes_accessed=0, transcendentals=0) if flops else None,
    )(*args)


def forward(x, hop):
    n = lax.axis_size("col")
    return lax.ppermute(x, "col", [(i, (i + hop) % n) for i in range(n)])


def swapped(x, axis, mask):
    return lax.ppermute(x, axis, [(i, i ^ mask) for i in range(lax.axis_size(axis))])


def row_parts(x):
    return [x] + [swapped(x, "row", m) for m in range(1, lax.axis_size("row"))]


def most_of_col(x):
    n, rows = lax.axis_size("col"), lax.axis_size("row")
    mask = RADIX
    while mask < n:
        x = jnp.maximum(x, swapped(x, "col", mask))
        mask *= 2
    near = min(n, RADIX) - 1
    each = -(-near // rows)
    seen = []
    for j in range(each):
        route = [
            (c * rows + r, (c ^ min(1 + r * each + j, near)) * rows + r)
            for r in range(rows) for c in range(n)
        ]
        seen.append(lax.ppermute(x, ("col", "row"), route))
    return functools.reduce(jnp.maximum, seen, x)


def to_pairs(weighted):
    n = lax.axis_size("col")
    if n > RADIX:
        whole = lax.all_to_all(weighted, "col", split_axis=1, concat_axis=0, tiled=True)
        return [whole], jnp.zeros((1,), jnp.int32)
    me = lax.axis_index("col")
    days, width = weighted.shape[0], weighted.shape[1] // n
    blocks = []
    for mask in range(n):
        block = lax.dynamic_slice(weighted, (0, (me ^ mask) * width), (days, width))
        blocks.append(swapped(block, "col", mask) if mask else block)
    return blocks, me ^ jnp.arange(n, dtype=jnp.int32)


def on_device(returns, counts, partner_shift):
    n, rows = lax.axis_size("col"), lax.axis_size("row")
    total_days = returns.shape[0] * n * rows
    mine = total_days // rows
    weighted = returns.astype(F32) * jnp.sqrt(counts.astype(F32))[:, None]
    blocks, at = to_pairs(weighted)
    block, gram_shape, tile = (mine, BW), (BW + TILE, BW), (TILE, BW)
    lead = mine // 2
    first, second, gram = call(
        gather_kernel, [block, block, gram_shape], at, *blocks, smem_in=1
    )
    strides = [1]
    while strides[-1] * RADIX < n:
        strides.append(strides[-1] * RADIX)
    lowest = 1 if len(strides) == 1 else 0
    tops = []
    for rnd in range(ROUNDS):
        coupling, measure = call(
            functools.partial(couple_kernel, float(total_days)), [(BW, BW), tile], *row_parts(gram)
        )

        def settle(early, first, top):
            return call(early_kernel, [(BW, BW), (lead, BW), gram_shape], early, first, top)

        early, = call(early_mix_kernel, [(BW + lead, BW)], coupling, first, second)

        def move(hop, first, second, coupling, measure, early):
            early = forward(early, hop) if hop else early
            late, = call(late_mix_kernel, [(mine - lead, BW)], coupling, first, second)
            late = forward(late, hop) if hop else late
            part = most_of_col(measure)
            kept, top = call(
                keep_kernel, [block, tile], *row_parts(part), coupling, first, second,
                flops=LONG,
            )
            early = settle(early, kept, top) if len(strides) == 1 else early
            return kept, early, late, top

        amount = partner_shift[rnd]
        branches = [functools.partial(move, hop) for hop in range(lowest, min(n, RADIX))]
        first, early, late, top = lax.switch(
            amount % RADIX - lowest, branches, first, second, coupling, measure, early
        )
        for stride in strides[1:]:
            routes = [lambda *xs: xs] + [
                lambda *xs, hop=hop: tuple(forward(x, hop * stride) for x in xs)
                for hop in range(1, min(RADIX, n // stride))
            ]
            early, late = lax.switch(amount // stride % RADIX, routes, early, late)
        factor, start, gram = early if len(strides) == 1 else settle(early, first, top)
        tops.append(top)
        if rnd < ROUNDS - 1:
            second, gram = call(late_kernel, [block, gram_shape], late, factor, first, start, gram)
    return tuple(
        call(last_kernel, [(mine, 2 * BW), (ROUNDS,)], late, factor, first, start, *tops, smem_out=1)
    )


def solution(mesh):
    placed = (P(("row", "col"), None), P(("row", "col")), P())
    return jax.shard_map(
        on_device, mesh=mesh, in_specs=placed, out_specs=(P("row", "col"), P()), check_vma=False
    )
```

```python
import functools

import jax
import jax.numpy as jnp
from jax import lax
from jax.experimental import pallas as pl
from jax.experimental.pallas import tpu as pltpu
from jax.sharding import PartitionSpec as P

BW = 128
ROUNDS = 3
RADIX = 8
TILE = 8
LONG = 3 << 30
STEP = 256
F32 = jnp.float32


def split(x):
    high = x.astype(jnp.bfloat16)
    return high, (x - high.astype(F32)).astype(jnp.bfloat16)


def dot(a, b, dims=((1,), (0,))):
    one = functools.partial(
        lax.dot_general, dimension_numbers=(dims, ((), ())), preferred_element_type=F32
    )
    return one(a[0], b[0]) + (one(a[0], b[1]) + one(a[1], b[0]))


def dots(a, b, dims=((1,), (0,))):
    return dot(split(a), split(b), dims)


def unit():
    rows = lax.broadcasted_iota(jnp.int32, (BW, BW), 0)
    return (rows == lax.broadcasted_iota(jnp.int32, (BW, BW), 1)).astype(F32)


def polar(m, top):
    eye = unit()
    square = 1.0 / (1.0 + top)
    gram, product = square * (eye + m), None
    for turn in range(3):
        factor = 1.5 * eye - 0.5 * gram
        cut = split(factor)
        product = factor if product is None else dot(split(product), cut)
        if turn < 2:
            gram = dot(split(gram), split(dot(cut, cut)))
    return jnp.sqrt(square) * product


def steps(size, body):
    @pl.loop(0, size // STEP)
    def _(i):
        body(i * STEP, pl.ds(pl.multiple_of(i * STEP, STEP), STEP))


def gram_into(first, second, gram_ref):
    gram_ref[:BW] += dots(first, second, ((0,), (0,)))
    gram_ref[BW:BW + 1] += jnp.sum(first * first, 0, keepdims=True)
    gram_ref[BW + 1:BW + 2] += jnp.sum(second * second, 0, keepdims=True)


def gather_kernel(at_ref, *refs):
    blocks, (first_ref, second_ref, gram_ref) = refs[:-3], refs[-3:]
    days = blocks[0].shape[0]
    for i, block in enumerate(blocks):
        place = pl.ds(pl.multiple_of(at_ref[i] * days, TILE), days)
        first_ref[place] = block[:, :BW]
        second_ref[place] = block[:, BW:]
    gram_ref[...] = jnp.zeros_like(gram_ref)
    gram_into(first_ref[...], second_ref[...], gram_ref)


def couple_kernel(total_days, g0, g1, g2, g3, first, second, coupling_ref, measure_ref, early_ref):
    summed = (g0[...] + g1[...]) + (g2[...] + g3[...])
    norms = jnp.sqrt(summed[BW:BW + 2] / total_days + 1e-06)
    across = jnp.broadcast_to(norms[1:2], (BW, BW))
    down = jnp.broadcast_to(norms[0:1], (BW, BW)).T
    coupling = summed[:BW] / (total_days * down * across)
    measure_ref[...] = jnp.full((TILE, BW), jnp.sum(coupling * coupling), F32)
    coupling_ref[...] = coupling
    lead = early_ref.shape[0] - BW
    early_ref[:BW] = coupling
    early_ref[BW:] = dots(first[:lead], coupling) + second[:lead]


def late_mix_kernel(coupling, first, second, late_ref):
    lead = first.shape[0] - late_ref.shape[0]
    cut = split(coupling[...])

    def body(at, here):
        there = pl.ds(pl.multiple_of(lead + at, STEP), STEP)
        late_ref[here] = dot(split(first[there]), cut) + second[there]

    steps(late_ref.shape[0], body)


def keep_kernel(m0, m1, m2, m3, coupling, first, second, tops, first_ref, tops_ref):
    top = jnp.maximum(jnp.maximum(m0[...], m1[...]), jnp.maximum(m2[...], m3[...]))[:1]
    tops_ref[:1] = top
    tops_ref[1:] = tops[:TILE - 1]
    cut = split(coupling[...])
    factor = polar(dot(cut, cut, ((1,), (1,))), top)
    weight = split(factor)
    other = split(dot(cut, weight, ((0,), (0,))))

    def body(_, here):
        first_ref[here] = dot(split(first[here]), weight) - dot(split(second[here]), other)

    steps(first.shape[0], body)


def early_kernel(early, first, tops, factor_ref, second_ref, gram_ref):
    cut = split(early[:BW])
    factor = polar(dot(cut, cut, ((0,), (0,))), tops[:1])
    factor_ref[...] = factor
    weight = split(factor)
    gram_ref[...] = jnp.zeros_like(gram_ref)

    def body(at, here):
        there = pl.ds(pl.multiple_of(BW + at, BW), STEP)
        second_ref[here] = dot(split(early[there]), weight)
        gram_into(first[here], second_ref[here], gram_ref)

    steps(second_ref.shape[0], body)


def late_kernel(late, factor, first, lead, gram, second_ref, gram_ref):
    second = dots(late[...], factor[...])
    size = lead.shape[0]
    second_ref[:size] = lead[...]
    second_ref[size:] = second
    gram_ref[...] = gram[...]
    gram_into(first[size:], second, gram_ref)


def last_kernel(first, second, tops, out_ref, bounds_ref):
    out_ref[:, :BW] = first[...]
    out_ref[:, BW:] = second[...]
    for i in range(ROUNDS):
        bounds_ref[i] = tops[ROUNDS - 1 - i, 0]


def call(kernel, outs, *args, smem_in=0, smem_out=0, flops=0):
    vmem, smem = pl.BlockSpec(memory_space=pltpu.VMEM), pl.BlockSpec(memory_space=pltpu.SMEM)
    shapes = [jax.ShapeDtypeStruct(s, F32) for s in outs]
    return pl.pallas_call(
        kernel,
        out_shape=shapes,
        in_specs=[smem] * smem_in + [vmem] * (len(args) - smem_in),
        out_specs=[vmem] * (len(outs) - smem_out) + [smem] * smem_out,
        compiler_params=pltpu.CompilerParams(vmem_limit_bytes=24 << 20),
        cost_estimate=pl.CostEstimate(flops=flops, bytes_accessed=0, transcendentals=0) if flops else None,
    )(*args)


def forward(x, hop):
    n = lax.axis_size("col")
    return lax.ppermute(x, "col", [(i, (i + hop) % n) for i in range(n)])


def swapped(x, axis, mask):
    return lax.ppermute(x, axis, [(i, i ^ mask) for i in range(lax.axis_size(axis))])


def row_parts(x):
    return [x] + [swapped(x, "row", m) for m in range(1, lax.axis_size("row"))]


def most_of_col(x):
    n, rows = lax.axis_size("col"), lax.axis_size("row")
    mask = RADIX
    while mask < n:
        x = jnp.maximum(x, swapped(x, "col", mask))
        mask *= 2
    near = min(n, RADIX) - 1
    each = -(-near // rows)
    seen = []
    for j in range(each):
        route = [
            (c * rows + r, (c ^ min(1 + r * each + j, near)) * rows + r)
            for r in range(rows) for c in range(n)
        ]
        seen.append(lax.ppermute(x, ("col", "row"), route))
    return functools.reduce(jnp.maximum, seen, x)


def to_pairs(weighted):
    n = lax.axis_size("col")
    if n > RADIX:
        whole = lax.all_to_all(weighted, "col", split_axis=1, concat_axis=0, tiled=True)
        return [whole], jnp.zeros((1,), jnp.int32)
    me = lax.axis_index("col")
    days, width = weighted.shape[0], weighted.shape[1] // n
    blocks = []
    for mask in range(n):
        block = lax.dynamic_slice(weighted, (0, (me ^ mask) * width), (days, width))
        blocks.append(swapped(block, "col", mask) if mask else block)
    return blocks, me ^ jnp.arange(n, dtype=jnp.int32)


def on_device(returns, counts, partner_shift):
    n, rows = lax.axis_size("col"), lax.axis_size("row")
    total_days = returns.shape[0] * n * rows
    mine = total_days // rows
    weighted = returns.astype(F32) * jnp.sqrt(counts.astype(F32))[:, None]
    blocks, at = to_pairs(weighted)
    block, gram_shape, tile = (mine, BW), (BW + TILE, BW), (TILE, BW)
    lead = mine // 2
    first, second, gram = call(
        gather_kernel, [block, block, gram_shape], at, *blocks, smem_in=1
    )
    strides = [1]
    while strides[-1] * RADIX < n:
        strides.append(strides[-1] * RADIX)
    lowest = 1 if len(strides) == 1 else 0

    def settle(early, first, tops):
        return call(early_kernel, [(BW, BW), (lead, BW), gram_shape], early, first, tops)

    def move(hop, first, second, coupling, measure, early, tops):
        early = forward(early, hop) if hop else early
        late, = call(late_mix_kernel, [(mine - lead, BW)], coupling, first, second)
        late = forward(late, hop) if hop else late
        part = most_of_col(measure)
        kept, tops = call(
            keep_kernel, [block, tile], *row_parts(part), coupling, first, second, tops, flops=LONG
        )
        early = settle(early, kept, tops) if len(strides) == 1 else early
        return kept, early, late, tops

    def one_round(carry, amount):
        first, second, gram, tops = carry
        coupling, measure, early = call(
            functools.partial(couple_kernel, float(total_days)), [(BW, BW), tile, (BW + lead, BW)],
            *row_parts(gram), first, second,
        )
        branches = [functools.partial(move, hop) for hop in range(lowest, min(n, RADIX))]
        first, early, late, tops = lax.switch(
            amount % RADIX - lowest, branches, first, second, coupling, measure, early, tops
        )
        for stride in strides[1:]:
            routes = [lambda *xs: xs] + [
                lambda *xs, hop=hop: tuple(forward(x, hop * stride) for x in xs)
                for hop in range(1, min(RADIX, n // stride))
            ]
            early, late = lax.switch(amount // stride % RADIX, routes, early, late)
        factor, start, gram = early if len(strides) == 1 else settle(early, first, tops)
        second, gram = call(late_kernel, [block, gram_shape], late, factor, first, start, gram)
        return (first, second, gram, tops), None

    tops = jnp.zeros(tile, F32)
    (first, second, _, tops), _ = lax.scan(one_round, (first, second, gram, tops), partner_shift)
    return tuple(
        call(last_kernel, [(mine, 2 * BW), (ROUNDS,)], first, second, tops, smem_out=1)
    )


def solution(mesh):
    placed = (P(("row", "col"), None), P(("row", "col")), P())
    return jax.shard_map(
        on_device, mesh=mesh, in_specs=placed, out_specs=(P("row", "col"), P()), check_vma=False
    )
```

```python
import functools

import jax
import jax.numpy as jnp
from jax import lax
from jax.experimental import pallas as pl
from jax.experimental.pallas import tpu as pltpu
from jax.sharding import PartitionSpec as P

BW = 128
ROUNDS = 3
RADIX = 8
TILE = 8
LONG = 3 << 30
STEP = 256
F32 = jnp.float32


def split(x):
    high = x.astype(jnp.bfloat16)
    return high, (x - high.astype(F32)).astype(jnp.bfloat16)


def dot(a, b, dims=((1,), (0,))):
    one = functools.partial(
        lax.dot_general, dimension_numbers=(dims, ((), ())), preferred_element_type=F32
    )
    return one(a[0], b[0]) + (one(a[0], b[1]) + one(a[1], b[0]))


def dots(a, b, dims=((1,), (0,))):
    return dot(split(a), split(b), dims)


def unit():
    rows = lax.broadcasted_iota(jnp.int32, (BW, BW), 0)
    return (rows == lax.broadcasted_iota(jnp.int32, (BW, BW), 1)).astype(F32)


def polar(m, top):
    eye = unit()
    square = 1.0 / (1.0 + top)
    gram, product = square * (eye + m), None
    for turn in range(3):
        factor = 1.5 * eye - 0.5 * gram
        cut = split(factor)
        product = factor if product is None else dot(split(product), cut)
        if turn < 2:
            gram = dot(split(gram), split(dot(cut, cut)))
    return jnp.sqrt(square) * product


def steps(size, body):
    @pl.loop(0, size // STEP)
    def _(i):
        body(i * STEP, pl.ds(pl.multiple_of(i * STEP, STEP), STEP))


def gram_into(first, second, gram_ref):
    gram_ref[:BW] += dots(first, second, ((0,), (0,)))
    gram_ref[BW:BW + 1] += jnp.sum(first * first, 0, keepdims=True)
    gram_ref[BW + 1:BW + 2] += jnp.sum(second * second, 0, keepdims=True)


def gather_kernel(at_ref, *refs):
    blocks, (first_ref, second_ref, gram_ref) = refs[:-3], refs[-3:]
    days = blocks[0].shape[0]
    for i, block in enumerate(blocks):
        place = pl.ds(pl.multiple_of(at_ref[i] * days, TILE), days)
        first_ref[place] = block[:, :BW]
        second_ref[place] = block[:, BW:]
    gram_ref[...] = jnp.zeros_like(gram_ref)
    gram_into(first_ref[...], second_ref[...], gram_ref)


def couple_kernel(total_days, g0, g1, g2, g3, first, second, coupling_ref, measure_ref, early_ref):
    summed = (g0[...] + g1[...]) + (g2[...] + g3[...])
    norms = jnp.sqrt(summed[BW:BW + 2] / total_days + 1e-06)
    across = jnp.broadcast_to(norms[1:2], (BW, BW))
    down = jnp.broadcast_to(norms[0:1], (BW, BW)).T
    coupling = summed[:BW] / (total_days * down * across)
    measure_ref[...] = jnp.full((TILE, BW), jnp.sum(coupling * coupling), F32)
    coupling_ref[...] = coupling
    lead = early_ref.shape[0] - BW
    early_ref[:BW] = coupling
    early_ref[BW:] = dots(first[:lead], coupling) + second[:lead]


def late_mix_kernel(coupling, first, second, late_ref):
    lead = first.shape[0] - late_ref.shape[0]
    cut = split(coupling[...])

    def body(at, here):
        there = pl.ds(pl.multiple_of(lead + at, STEP), STEP)
        late_ref[here] = dot(split(first[there]), cut) + second[there]

    steps(late_ref.shape[0], body)


def keep_kernel(m0, m1, m2, m3, coupling, first, second, tops, first_ref, tops_ref):
    top = jnp.maximum(jnp.maximum(m0[...], m1[...]), jnp.maximum(m2[...], m3[...]))[:1]
    tops_ref[:1] = top
    tops_ref[1:] = tops[:TILE - 1]
    cut = split(coupling[...])
    factor = polar(dot(cut, cut, ((1,), (1,))), top)
    weight = split(factor)
    other = split(dot(cut, weight, ((0,), (0,))))

    def body(_, here):
        first_ref[here] = dot(split(first[here]), weight) - dot(split(second[here]), other)

    steps(first.shape[0], body)


def early_kernel(early, first, tops, factor_ref, second_ref, gram_ref):
    cut = split(early[:BW])
    factor = polar(dot(cut, cut, ((0,), (0,))), tops[:1])
    factor_ref[...] = factor
    weight = split(factor)
    gram_ref[...] = jnp.zeros_like(gram_ref)

    def body(at, here):
        there = pl.ds(pl.multiple_of(BW + at, BW), STEP)
        second_ref[here] = dot(split(early[there]), weight)
        gram_into(first[here], second_ref[here], gram_ref)

    steps(second_ref.shape[0], body)


def late_kernel(late, factor, first, lead, tops, first_ref, second_ref, gram_ref, tops_ref):
    second = dots(late[...], factor[...])
    size = lead.shape[0]
    first_ref[...] = first[...]
    tops_ref[...] = tops[...]
    second_ref[:size] = lead[...]
    second_ref[size:] = second
    gram_ref[...] = jnp.zeros_like(gram_ref)
    gram_into(first[size:], second, gram_ref)


def last_kernel(first, second, tops, out_ref, bounds_ref):
    out_ref[:, :BW] = first[...]
    out_ref[:, BW:] = second[...]
    for i in range(ROUNDS):
        bounds_ref[i] = tops[ROUNDS - 1 - i, 0]


def call(kernel, outs, *args, smem_in=0, smem_out=0, flops=0):
    vmem, smem = pl.BlockSpec(memory_space=pltpu.VMEM), pl.BlockSpec(memory_space=pltpu.SMEM)
    shapes = [jax.ShapeDtypeStruct(s, F32) for s in outs]
    return pl.pallas_call(
        kernel,
        out_shape=shapes,
        in_specs=[smem] * smem_in + [vmem] * (len(args) - smem_in),
        out_specs=[vmem] * (len(outs) - smem_out) + [smem] * smem_out,
        compiler_params=pltpu.CompilerParams(vmem_limit_bytes=24 << 20),
        cost_estimate=pl.CostEstimate(flops=flops, bytes_accessed=0, transcendentals=0) if flops else None,
    )(*args)


def forward(x, hop):
    n = lax.axis_size("col")
    return lax.ppermute(x, "col", [(i, (i + hop) % n) for i in range(n)])


def swapped(x, axis, mask):
    return lax.ppermute(x, axis, [(i, i ^ mask) for i in range(lax.axis_size(axis))])


def row_parts(x):
    return [x] + [swapped(x, "row", m) for m in range(1, lax.axis_size("row"))]


def most_of_col(x):
    n, rows = lax.axis_size("col"), lax.axis_size("row")
    mask = RADIX
    while mask < n:
        x = jnp.maximum(x, swapped(x, "col", mask))
        mask *= 2
    near = min(n, RADIX) - 1
    each = -(-near // rows)
    seen = []
    for j in range(each):
        route = [
            (c * rows + r, (c ^ min(1 + r * each + j, near)) * rows + r)
            for r in range(rows) for c in range(n)
        ]
        seen.append(lax.ppermute(x, ("col", "row"), route))
    return functools.reduce(jnp.maximum, seen, x)


def to_pairs(weighted):
    n = lax.axis_size("col")
    if n > RADIX:
        whole = lax.all_to_all(weighted, "col", split_axis=1, concat_axis=0, tiled=True)
        return [whole], jnp.zeros((1,), jnp.int32)
    me = lax.axis_index("col")
    days, width = weighted.shape[0], weighted.shape[1] // n
    blocks = []
    for mask in range(n):
        block = lax.dynamic_slice(weighted, (0, (me ^ mask) * width), (days, width))
        blocks.append(swapped(block, "col", mask) if mask else block)
    return blocks, me ^ jnp.arange(n, dtype=jnp.int32)


def on_device(returns, counts, partner_shift):
    n, rows = lax.axis_size("col"), lax.axis_size("row")
    total_days = returns.shape[0] * n * rows
    mine = total_days // rows
    weighted = returns.astype(F32) * jnp.sqrt(counts.astype(F32))[:, None]
    blocks, at = to_pairs(weighted)
    block, gram_shape, tile = (mine, BW), (BW + TILE, BW), (TILE, BW)
    lead = mine // 2
    first, second, gram = call(
        gather_kernel, [block, block, gram_shape], at, *blocks, smem_in=1
    )
    strides = [1]
    while strides[-1] * RADIX < n:
        strides.append(strides[-1] * RADIX)
    lowest = 1 if len(strides) == 1 else 0

    def settle(early, late, first, tops):
        factor, start, gram = call(
            early_kernel, [(BW, BW), (lead, BW), gram_shape], early, first, tops
        )
        first, second, rest, tops = call(
            late_kernel, [block, block, gram_shape, tile], late, factor, first, start, tops
        )
        return first, second, gram, rest, tops

    def move(hop, first, second, coupling, measure, early, tops):
        early = forward(early, hop) if hop else early
        late, = call(late_mix_kernel, [(mine - lead, BW)], coupling, first, second)
        late = forward(late, hop) if hop else late
        part = most_of_col(measure)
        kept, tops = call(
            keep_kernel, [block, tile], *row_parts(part), coupling, first, second, tops, flops=LONG
        )
        if len(strides) == 1:
            return settle(early, late, kept, tops)
        return kept, early, late, tops

    def joined(first, second, gram, rest, tops):
        return first, second, gram + rest, tops

    def one_round(carry, amount):
        first, second, gram, tops = carry
        coupling, measure, early = call(
            functools.partial(couple_kernel, float(total_days)), [(BW, BW), tile, (BW + lead, BW)],
            *row_parts(gram), first, second,
        )
        branches = [functools.partial(move, hop) for hop in range(lowest, min(n, RADIX))]
        moved = lax.switch(
            amount % RADIX - lowest, branches, first, second, coupling, measure, early, tops
        )
        if len(strides) == 1:
            return joined(*moved), None
        first, early, late, tops = moved
        for stride in strides[1:]:
            routes = [lambda *xs: xs] + [
                lambda *xs, hop=hop: tuple(forward(x, hop * stride) for x in xs)
                for hop in range(1, min(RADIX, n // stride))
            ]
            early, late = lax.switch(amount // stride % RADIX, routes, early, late)
        return joined(*settle(early, late, first, tops)), None

    tops = jnp.zeros(tile, F32)
    (first, second, _, tops), _ = lax.scan(one_round, (first, second, gram, tops), partner_shift)
    return tuple(
        call(last_kernel, [(mine, 2 * BW), (ROUNDS,)], first, second, tops, smem_out=1)
    )


def solution(mesh):
    placed = (P(("row", "col"), None), P(("row", "col")), P())
    return jax.shard_map(
        on_device, mesh=mesh, in_specs=placed, out_specs=(P("row", "col"), P()), check_vma=False
    )
```

```python
import functools

import jax
import jax.numpy as jnp
from jax import lax
from jax.experimental import pallas as pl
from jax.experimental.pallas import tpu as pltpu
from jax.sharding import PartitionSpec as P

BW = 128
ROUNDS = 3
RADIX = 8
TILE = 8
LONG = 3 << 30
STEP = 256
F32 = jnp.float32


def split(x):
    high = x.astype(jnp.bfloat16)
    return high, (x - high.astype(F32)).astype(jnp.bfloat16)


def dot(a, b, dims=((1,), (0,))):
    one = functools.partial(
        lax.dot_general, dimension_numbers=(dims, ((), ())), preferred_element_type=F32
    )
    return one(a[0], b[0]) + (one(a[0], b[1]) + one(a[1], b[0]))


def dots(a, b, dims=((1,), (0,))):
    return dot(split(a), split(b), dims)


def unit():
    rows = lax.broadcasted_iota(jnp.int32, (BW, BW), 0)
    return (rows == lax.broadcasted_iota(jnp.int32, (BW, BW), 1)).astype(F32)


def polar(m, top):
    eye = unit()
    square = 1.0 / (1.0 + top)
    gram, product = square * (eye + m), None
    for turn in range(3):
        factor = 1.5 * eye - 0.5 * gram
        cut = split(factor)
        product = factor if product is None else dot(split(product), cut)
        if turn < 2:
            gram = dot(split(gram), split(dot(cut, cut)))
    return jnp.sqrt(square) * product


def steps(size, body):
    @pl.loop(0, size // STEP)
    def _(i):
        body(i * STEP, pl.ds(pl.multiple_of(i * STEP, STEP), STEP))


def gram_into(first, second, gram_ref):
    gram_ref[:BW] += dots(first, second, ((0,), (0,)))
    gram_ref[BW:BW + 1] += jnp.sum(first * first, 0, keepdims=True)
    gram_ref[BW + 1:BW + 2] += jnp.sum(second * second, 0, keepdims=True)


def gather_kernel(at_ref, *refs):
    blocks, (first_ref, second_ref, gram_ref) = refs[:-3], refs[-3:]
    days = blocks[0].shape[0]
    for i, block in enumerate(blocks):
        place = pl.ds(pl.multiple_of(at_ref[i] * days, TILE), days)
        first_ref[place] = block[:, :BW]
        second_ref[place] = block[:, BW:]
    gram_ref[...] = jnp.zeros_like(gram_ref)
    gram_into(first_ref[...], second_ref[...], gram_ref)


def couple_kernel(total_days, g0, g1, first, second, coupling_ref, measure_ref, early_ref):
    summed = g0[...] + g1[...]
    norms = jnp.sqrt(summed[BW:BW + 2] / total_days + 1e-06)
    across = jnp.broadcast_to(norms[1:2], (BW, BW))
    down = jnp.broadcast_to(norms[0:1], (BW, BW)).T
    coupling = summed[:BW] / (total_days * down * across)
    measure_ref[...] = jnp.full((TILE, BW), jnp.sum(coupling * coupling), F32)
    coupling_ref[...] = coupling
    lead = early_ref.shape[0] - BW
    early_ref[:BW] = coupling
    early_ref[BW:] = dots(first[:lead], coupling) + second[:lead]


def late_mix_kernel(coupling, first, second, late_ref):
    lead = first.shape[0] - late_ref.shape[0]
    cut = split(coupling[...])

    def body(at, here):
        there = pl.ds(pl.multiple_of(lead + at, STEP), STEP)
        late_ref[here] = dot(split(first[there]), cut) + second[there]

    steps(late_ref.shape[0], body)


def keep_kernel(m0, m1, m2, m3, coupling, first, second, tops, first_ref, tops_ref):
    top = jnp.maximum(jnp.maximum(m0[...], m1[...]), jnp.maximum(m2[...], m3[...]))[:1]
    tops_ref[:1] = top
    tops_ref[1:] = tops[:TILE - 1]
    cut = split(coupling[...])
    factor = polar(dot(cut, cut, ((1,), (1,))), top)
    weight = split(factor)
    other = split(dot(cut, weight, ((0,), (0,))))

    def body(_, here):
        first_ref[here] = dot(split(first[here]), weight) - dot(split(second[here]), other)

    steps(first.shape[0], body)


def early_kernel(early, first, tops, factor_ref, second_ref, gram_ref):
    cut = split(early[:BW])
    factor = polar(dot(cut, cut, ((0,), (0,))), tops[:1])
    factor_ref[...] = factor
    weight = split(factor)
    gram_ref[...] = jnp.zeros_like(gram_ref)

    def body(at, here):
        there = pl.ds(pl.multiple_of(BW + at, BW), STEP)
        second_ref[here] = dot(split(early[there]), weight)
        gram_into(first[here], second_ref[here], gram_ref)

    steps(second_ref.shape[0], body)


def late_kernel(late, factor, first, lead, tops, first_ref, second_ref, gram_ref, tops_ref):
    second = dots(late[...], factor[...])
    size = lead.shape[0]
    first_ref[...] = first[...]
    tops_ref[...] = tops[...]
    second_ref[:size] = lead[...]
    second_ref[size:] = second
    gram_ref[...] = jnp.zeros_like(gram_ref)
    gram_into(first[size:], second, gram_ref)


def last_kernel(first, second, tops, out_ref, bounds_ref):
    out_ref[:, :BW] = first[...]
    out_ref[:, BW:] = second[...]
    for i in range(ROUNDS):
        bounds_ref[i] = tops[ROUNDS - 1 - i, 0]


def call(kernel, outs, *args, smem_in=0, smem_out=0, flops=0):
    vmem, smem = pl.BlockSpec(memory_space=pltpu.VMEM), pl.BlockSpec(memory_space=pltpu.SMEM)
    shapes = [jax.ShapeDtypeStruct(s, F32) for s in outs]
    return pl.pallas_call(
        kernel,
        out_shape=shapes,
        in_specs=[smem] * smem_in + [vmem] * (len(args) - smem_in),
        out_specs=[vmem] * (len(outs) - smem_out) + [smem] * smem_out,
        compiler_params=pltpu.CompilerParams(vmem_limit_bytes=24 << 20),
        cost_estimate=pl.CostEstimate(flops=flops, bytes_accessed=0, transcendentals=0) if flops else None,
    )(*args)


def forward(x, hop):
    n = lax.axis_size("col")
    return lax.ppermute(x, "col", [(i, (i + hop) % n) for i in range(n)])


def swapped(x, axis, mask):
    return lax.ppermute(x, axis, [(i, i ^ mask) for i in range(lax.axis_size(axis))])


def row_parts(x):
    return [x] + [swapped(x, "row", m) for m in range(1, lax.axis_size("row"))]


def halves(x):
    mask = 1
    while 2 * mask < lax.axis_size("row"):
        x = x + swapped(x, "row", mask)
        mask *= 2
    return x, swapped(x, "row", mask)


def most_of_col(x):
    n, rows = lax.axis_size("col"), lax.axis_size("row")
    mask = RADIX
    while mask < n:
        x = jnp.maximum(x, swapped(x, "col", mask))
        mask *= 2
    near = min(n, RADIX) - 1
    each = -(-near // rows)
    seen = []
    for j in range(each):
        route = [
            (c * rows + r, (c ^ min(1 + r * each + j, near)) * rows + r)
            for r in range(rows) for c in range(n)
        ]
        seen.append(lax.ppermute(x, ("col", "row"), route))
    return functools.reduce(jnp.maximum, seen, x)


def to_pairs(weighted):
    n = lax.axis_size("col")
    if n > RADIX:
        whole = lax.all_to_all(weighted, "col", split_axis=1, concat_axis=0, tiled=True)
        return [whole], jnp.zeros((1,), jnp.int32)
    me = lax.axis_index("col")
    days, width = weighted.shape[0], weighted.shape[1] // n
    blocks = []
    for mask in range(n):
        block = lax.dynamic_slice(weighted, (0, (me ^ mask) * width), (days, width))
        blocks.append(swapped(block, "col", mask) if mask else block)
    return blocks, me ^ jnp.arange(n, dtype=jnp.int32)


def on_device(returns, counts, partner_shift):
    n, rows = lax.axis_size("col"), lax.axis_size("row")
    total_days = returns.shape[0] * n * rows
    mine = total_days // rows
    weighted = returns.astype(F32) * jnp.sqrt(counts.astype(F32))[:, None]
    blocks, at = to_pairs(weighted)
    block, gram_shape, tile = (mine, BW), (BW + TILE, BW), (TILE, BW)
    lead = mine // 2
    first, second, gram = call(
        gather_kernel, [block, block, gram_shape], at, *blocks, smem_in=1
    )
    strides = [1]
    while strides[-1] * RADIX < n:
        strides.append(strides[-1] * RADIX)
    lowest = 1 if len(strides) == 1 else 0

    def settle(early, late, first, tops):
        factor, start, gram = call(
            early_kernel, [(BW, BW), (lead, BW), gram_shape], early, first, tops
        )
        first, second, rest, tops = call(
            late_kernel, [block, block, gram_shape, tile], late, factor, first, start, tops
        )
        return first, second, gram, rest, tops

    def move(hop, first, second, coupling, measure, early, tops):
        early = forward(early, hop) if hop else early
        late, = call(late_mix_kernel, [(mine - lead, BW)], coupling, first, second)
        late = forward(late, hop) if hop else late
        part = most_of_col(measure)
        kept, tops = call(
            keep_kernel, [block, tile], *row_parts(part), coupling, first, second, tops, flops=LONG
        )
        if len(strides) == 1:
            return settle(early, late, kept, tops)
        return kept, early, late, tops

    def joined(first, second, gram, rest, tops):
        return first, second, gram + rest, tops

    def one_round(carry, amount):
        first, second, gram, tops = carry
        coupling, measure, early = call(
            functools.partial(couple_kernel, float(total_days)), [(BW, BW), tile, (BW + lead, BW)],
            *halves(gram), first, second,
        )
        branches = [functools.partial(move, hop) for hop in range(lowest, min(n, RADIX))]
        moved = lax.switch(
            amount % RADIX - lowest, branches, first, second, coupling, measure, early, tops
        )
        if len(strides) == 1:
            return joined(*moved), None
        first, early, late, tops = moved
        for stride in strides[1:]:
            routes = [lambda *xs: xs] + [
                lambda *xs, hop=hop: tuple(forward(x, hop * stride) for x in xs)
                for hop in range(1, min(RADIX, n // stride))
            ]
            early, late = lax.switch(amount // stride % RADIX, routes, early, late)
        return joined(*settle(early, late, first, tops)), None

    tops = jnp.zeros(tile, F32)
    (first, second, _, tops), _ = lax.scan(one_round, (first, second, gram, tops), partner_shift)
    return tuple(
        call(last_kernel, [(mine, 2 * BW), (ROUNDS,)], first, second, tops, smem_out=1)
    )


def solution(mesh):
    placed = (P(("row", "col"), None), P(("row", "col")), P())
    return jax.shard_map(
        on_device, mesh=mesh, in_specs=placed, out_specs=(P("row", "col"), P()), check_vma=False
    )
```

```python
import functools

import jax
import jax.numpy as jnp
from jax import lax
from jax.experimental import pallas as pl
from jax.experimental.pallas import tpu as pltpu
from jax.sharding import PartitionSpec as P

BW = 128
ROUNDS = 3
RADIX = 8
TILE = 8
LONG = 3 << 30
STEP = 256
F32 = jnp.float32


def split(x):
    high = x.astype(jnp.bfloat16)
    return high, (x - high.astype(F32)).astype(jnp.bfloat16)


def dot(a, b, dims=((1,), (0,))):
    one = functools.partial(
        lax.dot_general, dimension_numbers=(dims, ((), ())), preferred_element_type=F32
    )
    return one(a[0], b[0]) + (one(a[0], b[1]) + one(a[1], b[0]))


def dots(a, b, dims=((1,), (0,))):
    return dot(split(a), split(b), dims)


def unit():
    rows = lax.broadcasted_iota(jnp.int32, (BW, BW), 0)
    return (rows == lax.broadcasted_iota(jnp.int32, (BW, BW), 1)).astype(F32)


def polar(m, top):
    eye = unit()
    square = 1.0 / (1.0 + top)
    gram, product = square * (eye + m), None
    for turn in range(3):
        factor = 1.5 * eye - 0.5 * gram
        cut = split(factor)
        product = factor if product is None else dot(split(product), cut)
        if turn < 2:
            gram = dot(split(gram), split(dot(cut, cut)))
    return jnp.sqrt(square) * product


def steps(size, body):
    @pl.loop(0, size // STEP)
    def _(i):
        body(i * STEP, pl.ds(pl.multiple_of(i * STEP, STEP), STEP))


def gram_into(first, second, gram_ref):
    gram_ref[:BW] += dots(first, second, ((0,), (0,)))
    gram_ref[BW:BW + 1] += jnp.sum(first * first, 0, keepdims=True)
    gram_ref[BW + 1:BW + 2] += jnp.sum(second * second, 0, keepdims=True)


def gather_kernel(at_ref, *refs):
    blocks, (first_ref, second_ref, gram_ref) = refs[:-3], refs[-3:]
    days = blocks[0].shape[0]
    for i, block in enumerate(blocks):
        place = pl.ds(pl.multiple_of(at_ref[i] * days, TILE), days)
        first_ref[place] = block[:, :BW]
        second_ref[place] = block[:, BW:]
    gram_ref[...] = jnp.zeros_like(gram_ref)
    gram_into(first_ref[...], second_ref[...], gram_ref)


def couple_kernel(total_days, g0, g1, first, second, coupling_ref, measure_ref, early_ref):
    summed = g0[...] + g1[...]
    norms = jnp.sqrt(summed[BW:BW + 2] / total_days + 1e-06)
    across = jnp.broadcast_to(norms[1:2], (BW, BW))
    down = jnp.broadcast_to(norms[0:1], (BW, BW)).T
    coupling = summed[:BW] / (total_days * down * across)
    measure_ref[...] = jnp.full((TILE, BW), jnp.sum(coupling * coupling), F32)
    coupling_ref[...] = coupling
    lead = early_ref.shape[0] - BW
    early_ref[:BW] = coupling
    early_ref[BW:] = dots(first[:lead], coupling) + second[:lead]


def late_mix_kernel(coupling, first, second, late_ref):
    lead = first.shape[0] - late_ref.shape[0]
    cut = split(coupling[...])

    def body(at, here):
        there = pl.ds(pl.multiple_of(lead + at, STEP), STEP)
        late_ref[here] = dot(split(first[there]), cut) + second[there]

    steps(late_ref.shape[0], body)


def keep_kernel(m0, m1, coupling, first, second, tops, first_ref, tops_ref):
    top = jnp.maximum(m0[:1], m1[:1])
    tops_ref[:1] = top
    tops_ref[1:] = tops[:TILE - 1]
    cut = split(coupling[...])
    factor = polar(dot(cut, cut, ((1,), (1,))), top)
    weight = split(factor)
    other = split(dot(cut, weight, ((0,), (0,))))

    def body(_, here):
        first_ref[here] = dot(split(first[here]), weight) - dot(split(second[here]), other)

    steps(first.shape[0], body)


def early_kernel(early, first, tops, factor_ref, second_ref, gram_ref):
    cut = split(early[:BW])
    factor = polar(dot(cut, cut, ((0,), (0,))), tops[:1])
    factor_ref[...] = factor
    weight = split(factor)
    gram_ref[...] = jnp.zeros_like(gram_ref)

    def body(at, here):
        there = pl.ds(pl.multiple_of(BW + at, BW), STEP)
        second_ref[here] = dot(split(early[there]), weight)
        gram_into(first[here], second_ref[here], gram_ref)

    steps(second_ref.shape[0], body)


def late_kernel(late, factor, first, lead, tops, first_ref, second_ref, gram_ref, tops_ref):
    second = dots(late[...], factor[...])
    size = lead.shape[0]
    first_ref[...] = first[...]
    tops_ref[...] = tops[...]
    second_ref[:size] = lead[...]
    second_ref[size:] = second
    gram_ref[...] = jnp.zeros_like(gram_ref)
    gram_into(first[size:], second, gram_ref)


def last_kernel(first, second, tops, out_ref, bounds_ref):
    out_ref[:, :BW] = first[...]
    out_ref[:, BW:] = second[...]
    for i in range(ROUNDS):
        bounds_ref[i] = tops[ROUNDS - 1 - i, 0]


def call(kernel, outs, *args, smem_in=0, smem_out=0, flops=0):
    vmem, smem = pl.BlockSpec(memory_space=pltpu.VMEM), pl.BlockSpec(memory_space=pltpu.SMEM)
    shapes = [jax.ShapeDtypeStruct(s, F32) for s in outs]
    return pl.pallas_call(
        kernel,
        out_shape=shapes,
        in_specs=[smem] * smem_in + [vmem] * (len(args) - smem_in),
        out_specs=[vmem] * (len(outs) - smem_out) + [smem] * smem_out,
        compiler_params=pltpu.CompilerParams(vmem_limit_bytes=24 << 20),
        cost_estimate=pl.CostEstimate(flops=flops, bytes_accessed=0, transcendentals=0) if flops else None,
    )(*args)


def forward(x, hop):
    n = lax.axis_size("col")
    return lax.ppermute(x, "col", [(i, (i + hop) % n) for i in range(n)])


def swapped(x, axis, mask):
    return lax.ppermute(x, axis, [(i, i ^ mask) for i in range(lax.axis_size(axis))])


def halves(x, join):
    mask = 1
    while 2 * mask < lax.axis_size("row"):
        x = join(x, swapped(x, "row", mask))
        mask *= 2
    return x, swapped(x, "row", mask)


def most_of_col(x):
    n, rows = lax.axis_size("col"), lax.axis_size("row")
    mask = RADIX
    while mask < n:
        x = jnp.maximum(x, swapped(x, "col", mask))
        mask *= 2
    near = min(n, RADIX) - 1
    each = -(-near // rows)
    seen = []
    for j in range(each):
        route = [
            (c * rows + r, (c ^ min(1 + r * each + j, near)) * rows + r)
            for r in range(rows) for c in range(n)
        ]
        seen.append(lax.ppermute(x, ("col", "row"), route))
    return functools.reduce(jnp.maximum, seen, x)


def to_pairs(weighted):
    n = lax.axis_size("col")
    if n > RADIX:
        whole = lax.all_to_all(weighted, "col", split_axis=1, concat_axis=0, tiled=True)
        return [whole], jnp.zeros((1,), jnp.int32)
    me = lax.axis_index("col")
    days, width = weighted.shape[0], weighted.shape[1] // n
    blocks = []
    for mask in range(n):
        block = lax.dynamic_slice(weighted, (0, (me ^ mask) * width), (days, width))
        blocks.append(swapped(block, "col", mask) if mask else block)
    return blocks, me ^ jnp.arange(n, dtype=jnp.int32)


def on_device(returns, counts, partner_shift):
    n, rows = lax.axis_size("col"), lax.axis_size("row")
    total_days = returns.shape[0] * n * rows
    mine = total_days // rows
    weighted = returns.astype(F32) * jnp.sqrt(counts.astype(F32))[:, None]
    blocks, at = to_pairs(weighted)
    block, gram_shape, tile = (mine, BW), (BW + TILE, BW), (TILE, BW)
    lead = mine * 3 // 4
    first, second, gram = call(
        gather_kernel, [block, block, gram_shape], at, *blocks, smem_in=1
    )
    strides = [1]
    while strides[-1] * RADIX < n:
        strides.append(strides[-1] * RADIX)
    lowest = 1 if len(strides) == 1 else 0

    def settle(early, late, first, tops):
        factor, start, gram = call(
            early_kernel, [(BW, BW), (lead, BW), gram_shape], early, first, tops
        )
        first, second, rest, tops = call(
            late_kernel, [block, block, gram_shape, tile], late, factor, first, start, tops
        )
        return first, second, gram, rest, tops

    def move(hop, first, second, coupling, measure, early, tops):
        early = forward(early, hop) if hop else early
        late, = call(late_mix_kernel, [(mine - lead, BW)], coupling, first, second)
        late = forward(late, hop) if hop else late
        part = most_of_col(measure)
        kept, tops = call(
            keep_kernel, [block, tile], *halves(part, jnp.maximum), coupling, first, second, tops, flops=LONG
        )
        if len(strides) == 1:
            return settle(early, late, kept, tops)
        return kept, early, late, tops

    def joined(first, second, gram, rest, tops):
        return first, second, gram + rest, tops

    def one_round(carry, amount):
        first, second, gram, tops = carry
        coupling, measure, early = call(
            functools.partial(couple_kernel, float(total_days)), [(BW, BW), tile, (BW + lead, BW)],
            *halves(gram, jnp.add), first, second,
        )
        branches = [functools.partial(move, hop) for hop in range(lowest, min(n, RADIX))]
        moved = lax.switch(
            amount % RADIX - lowest, branches, first, second, coupling, measure, early, tops
        )
        if len(strides) == 1:
            return joined(*moved), None
        first, early, late, tops = moved
        for stride in strides[1:]:
            routes = [lambda *xs: xs] + [
                lambda *xs, hop=hop: tuple(forward(x, hop * stride) for x in xs)
                for hop in range(1, min(RADIX, n // stride))
            ]
            early, late = lax.switch(amount // stride % RADIX, routes, early, late)
        return joined(*settle(early, late, first, tops)), None

    tops = jnp.zeros(tile, F32)
    (first, second, _, tops), _ = lax.scan(one_round, (first, second, gram, tops), partner_shift)
    return tuple(
        call(last_kernel, [(mine, 2 * BW), (ROUNDS,)], first, second, tops, smem_out=1)
    )


def solution(mesh):
    placed = (P(("row", "col"), None), P(("row", "col")), P())
    return jax.shard_map(
        on_device, mesh=mesh, in_specs=placed, out_specs=(P("row", "col"), P()), check_vma=False
    )
```

```python
import functools

import jax
import jax.numpy as jnp
from jax import lax
from jax.experimental import pallas as pl
from jax.experimental.pallas import tpu as pltpu
from jax.sharding import PartitionSpec as P

BW = 128
ROUNDS = 3
RADIX = 8
TILE = 8
LONG = 3 << 30
STEP = 256
F32 = jnp.float32


def split(x):
    high = x.astype(jnp.bfloat16)
    return high, (x - high.astype(F32)).astype(jnp.bfloat16)


def dot(a, b, dims=((1,), (0,))):
    one = functools.partial(
        lax.dot_general, dimension_numbers=(dims, ((), ())), preferred_element_type=F32
    )
    return one(a[0], b[0]) + (one(a[0], b[1]) + one(a[1], b[0]))


def dots(a, b, dims=((1,), (0,))):
    return dot(split(a), split(b), dims)


def unit():
    rows = lax.broadcasted_iota(jnp.int32, (BW, BW), 0)
    return (rows == lax.broadcasted_iota(jnp.int32, (BW, BW), 1)).astype(F32)


def polar(m, top):
    eye = unit()
    square = 1.0 / (1.0 + top)
    gram, product = square * (eye + m), None
    for turn in range(3):
        factor = 1.5 * eye - 0.5 * gram
        cut = split(factor)
        product = factor if product is None else dot(split(product), cut)
        if turn < 2:
            gram = dot(split(gram), split(dot(cut, cut)))
    return jnp.sqrt(square) * product


def steps(size, body):
    @pl.loop(0, size // STEP)
    def _(i):
        body(i * STEP, pl.ds(pl.multiple_of(i * STEP, STEP), STEP))


def gram_into(first, second, gram_ref):
    gram_ref[:BW] += dots(first, second, ((0,), (0,)))
    gram_ref[BW:BW + 1] += jnp.sum(first * first, 0, keepdims=True)
    gram_ref[BW + 1:BW + 2] += jnp.sum(second * second, 0, keepdims=True)


def gather_kernel(at_ref, *refs):
    blocks, (first_ref, second_ref, gram_ref) = refs[:-3], refs[-3:]
    days = blocks[0].shape[0]
    for i, block in enumerate(blocks):
        place = pl.ds(pl.multiple_of(at_ref[i] * days, TILE), days)
        first_ref[place] = block[:, :BW]
        second_ref[place] = block[:, BW:]
    gram_ref[...] = jnp.zeros_like(gram_ref)
    gram_into(first_ref[...], second_ref[...], gram_ref)


def couple_kernel(total_days, g0, g1, first, second, coupling_ref, measure_ref, early_ref):
    summed = g0[...] + g1[...]
    norms = jnp.sqrt(summed[BW:BW + 2] / total_days + 1e-06)
    across = jnp.broadcast_to(norms[1:2], (BW, BW))
    down = jnp.broadcast_to(norms[0:1], (BW, BW)).T
    coupling = summed[:BW] / (total_days * down * across)
    measure_ref[...] = jnp.full((TILE, BW), jnp.sum(coupling * coupling), F32)
    coupling_ref[...] = coupling
    lead = early_ref.shape[0] - BW
    early_ref[:BW] = coupling
    early_ref[BW:] = dots(first[:lead], coupling) + second[:lead]


def late_mix_kernel(coupling, first, second, late_ref):
    lead = first.shape[0] - late_ref.shape[0]
    cut = split(coupling[...])

    def body(at, here):
        there = pl.ds(pl.multiple_of(lead + at, STEP), STEP)
        late_ref[here] = dot(split(first[there]), cut) + second[there]

    steps(late_ref.shape[0], body)


def keep_kernel(m0, m1, m2, m3, coupling, first, second, tops, first_ref, tops_ref):
    top = jnp.maximum(jnp.maximum(m0[...], m1[...]), jnp.maximum(m2[...], m3[...]))[:1]
    tops_ref[:1] = top
    tops_ref[1:] = tops[:TILE - 1]
    cut = split(coupling[...])
    factor = polar(dot(cut, cut, ((1,), (1,))), top)
    weight = split(factor)
    other = split(dot(cut, weight, ((0,), (0,))))

    def body(_, here):
        first_ref[here] = dot(split(first[here]), weight) - dot(split(second[here]), other)

    steps(first.shape[0], body)


def early_kernel(early, first, tops, factor_ref, second_ref, gram_ref):
    cut = split(early[:BW])
    factor = polar(dot(cut, cut, ((0,), (0,))), tops[:1])
    factor_ref[...] = factor
    weight = split(factor)
    gram_ref[...] = jnp.zeros_like(gram_ref)

    def body(at, here):
        there = pl.ds(pl.multiple_of(BW + at, BW), STEP)
        second_ref[here] = dot(split(early[there]), weight)
        gram_into(first[here], second_ref[here], gram_ref)

    steps(second_ref.shape[0], body)


def late_kernel(late, factor, first, lead, tops, first_ref, second_ref, gram_ref, tops_ref):
    second = dots(late[...], factor[...])
    size = lead.shape[0]
    first_ref[...] = first[...]
    tops_ref[...] = tops[...]
    second_ref[:size] = lead[...]
    second_ref[size:] = second
    gram_ref[...] = jnp.zeros_like(gram_ref)
    gram_into(first[size:], second, gram_ref)


def last_kernel(first, second, tops, out_ref, bounds_ref):
    out_ref[:, :BW] = first[...]
    out_ref[:, BW:] = second[...]
    for i in range(ROUNDS):
        bounds_ref[i] = tops[ROUNDS - 1 - i, 0]


def call(kernel, outs, *args, smem_in=0, smem_out=0, flops=0):
    vmem, smem = pl.BlockSpec(memory_space=pltpu.VMEM), pl.BlockSpec(memory_space=pltpu.SMEM)
    shapes = [jax.ShapeDtypeStruct(s, F32) for s in outs]
    return pl.pallas_call(
        kernel,
        out_shape=shapes,
        in_specs=[smem] * smem_in + [vmem] * (len(args) - smem_in),
        out_specs=[vmem] * (len(outs) - smem_out) + [smem] * smem_out,
        compiler_params=pltpu.CompilerParams(vmem_limit_bytes=24 << 20),
        cost_estimate=pl.CostEstimate(flops=flops, bytes_accessed=0, transcendentals=0) if flops else None,
    )(*args)


def forward(x, hop):
    n = lax.axis_size("col")
    return lax.ppermute(x, "col", [(i, (i + hop) % n) for i in range(n)])


def swapped(x, axis, mask):
    return lax.ppermute(x, axis, [(i, i ^ mask) for i in range(lax.axis_size(axis))])


def row_parts(x):
    return [x] + [swapped(x, "row", m) for m in range(1, lax.axis_size("row"))]


def halves(x):
    mask = 1
    while 2 * mask < lax.axis_size("row"):
        x = x + swapped(x, "row", mask)
        mask *= 2
    return x, swapped(x, "row", mask)


def most_of_col(x):
    n, rows = lax.axis_size("col"), lax.axis_size("row")
    mask = RADIX
    while mask < n:
        x = jnp.maximum(x, swapped(x, "col", mask))
        mask *= 2
    near = min(n, RADIX) - 1
    each = -(-near // rows)
    seen = []
    for j in range(each):
        route = [
            (c * rows + r, (c ^ min(1 + r * each + j, near)) * rows + r)
            for r in range(rows) for c in range(n)
        ]
        seen.append(lax.ppermute(x, ("col", "row"), route))
    return functools.reduce(jnp.maximum, seen, x)


def to_pairs(weighted):
    n = lax.axis_size("col")
    if n > RADIX:
        whole = lax.all_to_all(weighted, "col", split_axis=1, concat_axis=0, tiled=True)
        return [whole], jnp.zeros((1,), jnp.int32)
    me = lax.axis_index("col")
    days, width = weighted.shape[0], weighted.shape[1] // n
    blocks = []
    for mask in range(n):
        block = lax.dynamic_slice(weighted, (0, (me ^ mask) * width), (days, width))
        blocks.append(swapped(block, "col", mask) if mask else block)
    return blocks, me ^ jnp.arange(n, dtype=jnp.int32)


def on_device(returns, counts, partner_shift):
    n, rows = lax.axis_size("col"), lax.axis_size("row")
    total_days = returns.shape[0] * n * rows
    mine = total_days // rows
    weighted = returns.astype(F32) * jnp.sqrt(counts.astype(F32))[:, None]
    blocks, at = to_pairs(weighted)
    block, gram_shape, tile = (mine, BW), (BW + TILE, BW), (TILE, BW)
    lead = mine // 2
    first, second, gram = call(
        gather_kernel, [block, block, gram_shape], at, *blocks, smem_in=1
    )
    strides = [1]
    while strides[-1] * RADIX < n:
        strides.append(strides[-1] * RADIX)
    lowest = 1 if len(strides) == 1 else 0

    def settle(early, late, first, tops):
        factor, start, gram = call(
            early_kernel, [(BW, BW), (lead, BW), gram_shape], early, first, tops
        )
        first, second, rest, tops = call(
            late_kernel, [block, block, gram_shape, tile], late, factor, first, start, tops
        )
        return first, second, gram, rest, tops

    def move(hop, first, second, coupling, measure, early, tops):
        early = forward(early, hop) if hop else early
        late, = call(late_mix_kernel, [(mine - lead, BW)], coupling, first, second)
        late = forward(late, hop) if hop else late
        part = most_of_col(measure)
        kept, tops = call(
            keep_kernel, [block, tile], *row_parts(part), coupling, first, second, tops, flops=LONG
        )
        if len(strides) == 1:
            return settle(early, late, kept, tops)
        return kept, early, late, tops

    def joined(first, second, gram, rest, tops):
        return first, second, gram + rest, tops

    def one_round(carry, digits):
        first, second, gram, tops = carry
        coupling, measure, early = call(
            functools.partial(couple_kernel, float(total_days)), [(BW, BW), tile, (BW + lead, BW)],
            *halves(gram), first, second,
        )
        branches = [functools.partial(move, hop) for hop in range(lowest, min(n, RADIX))]
        moved = lax.switch(
            digits[0], branches, first, second, coupling, measure, early, tops
        )
        if len(strides) == 1:
            return joined(*moved), None
        first, early, late, tops = moved
        for digit, stride in zip(digits[1:], strides[1:]):
            routes = [lambda *xs: xs] + [
                lambda *xs, hop=hop: tuple(forward(x, hop * stride) for x in xs)
                for hop in range(1, min(RADIX, n // stride))
            ]
            early, late = lax.switch(digit, routes, early, late)
        return joined(*settle(early, late, first, tops)), None

    tops = jnp.zeros(tile, F32)
    digits = [partner_shift // stride % RADIX for stride in strides]
    digits[0] = digits[0] - lowest
    (first, second, _, tops), _ = lax.scan(one_round, (first, second, gram, tops), digits)
    return tuple(
        call(last_kernel, [(mine, 2 * BW), (ROUNDS,)], first, second, tops, smem_out=1)
    )


def solution(mesh):
    placed = (P(("row", "col"), None), P(("row", "col")), P())
    return jax.shard_map(
        on_device, mesh=mesh, in_specs=placed, out_specs=(P("row", "col"), P()), check_vma=False
    )
```
